32 devices in a mesh: groups: 2 (over y), rows: 4 (over z), cols: 4 (over x, core).
Axes of the slice: x: 2, y: 2, z: 4, core: 2. Of those that a mesh axis runs over, the one named last changes fastest.
Arguments:
- block_tiles: bfloat16 [8, 128, 256, 256], P(('groups', 'rows'), 'cols'), parts along dimension 0, may hold values from -0.0625 to 0.0625
- block_rows: int32 [8, 128], P(('groups', 'rows'), 'cols'), parts along dimension 0, may hold values from 0 to 31, as said below
- block_cols: int32 [8, 128], P(('groups', 'rows'), 'cols'), parts along dimension 0, may hold values from 0 to 31, as said below
- counts: int32 [8, 4], P(('groups', 'rows'), 'cols'), parts along dimension 0, may hold values from 16 to 32, as said below
- cell_order: int32 [8, 2048], P(('groups', 'rows')), parts along dimension 0, may hold values from 0 to 2047, each once within a row
- start_vectors: bfloat16 [16384, 128], P(('groups', 'rows')), parts along dimension 0, may hold values from 0 to 30
Outputs:
- encodings: float32 [16384, 128], P(('groups', 'rows', 'cols')), parts along dimension 0
The draws below stay inside these ranges and needn't reach their ends.
There are 2 independent parts, one for each index of `groups`. The reference program is written for one: setup_inputs(seed, part) draws one part's arguments, and reference() takes and returns one part's arrays. A program takes and returns all parts, laid end to end along the dimension named above; each array names one. Nothing has to cross between parts.
Inputs may be any that keep to these rules, and one draw needn't show every extreme that they name: Every stored block has block_rows <= block_cols, its block row among the 8 blocks of its own row index. Among the stored blocks of one device, at most 1 have a block column on the cells of any one other row index; every device of a lower row index has exactly that many on the last row index. `block_cols`: drawn together with block_rows. `counts`: the devices at row index 0 hold 32 live blocks.
All inputs are finite; a program needn't handle non-finite values.
Results may differ from the reference program's by a relative error of at most 0.0072.
Values may be sent and summed in bfloat16 or wider, within the bound.
A program may use at most 64 MiB of HBM per device.

```python
import math
import jax
import jax.numpy as jnp
from jax import lax

VECTORS = 128
BLOCK = 256
BLOCKS_DEV = 8
TILES_DEV = 32
SLOTS = 1
ITERS = 2
CELLS_DEV = 2048
N_ROWS = 4
N_COLS = 4


def block_pairs(key):
    key_spread = jax.random.fold_in(key, 11)
    key_first = jax.random.fold_in(key, 12)
    key_second = jax.random.fold_in(key, 13)
    shape = (N_ROWS, N_COLS, TILES_DEV)
    row_index = jnp.arange(N_ROWS, dtype=jnp.int32)[:, None, None]
    spread = jax.random.randint(key_spread, shape, 0, 1 << 20)
    offset = spread % (N_ROWS - row_index)
    first_slot = jnp.arange(TILES_DEV, dtype=jnp.int32)[None, None, :] == 0
    offset = jnp.where(first_slot, N_ROWS - 1 - row_index, offset)
    owner_row = row_index + offset
    remote = offset > 0
    peer_marks = ((owner_row[..., None] == jnp.arange(N_ROWS, dtype=jnp.int32)) & remote[..., None]).astype(jnp.int32)
    earlier = jnp.cumsum(peer_marks, axis=2) - peer_marks
    taken = jnp.sum(earlier * peer_marks, axis=-1)
    owner_row = jnp.where(remote & (taken >= SLOTS), row_index, owner_row)
    remote = owner_row != row_index
    first_pick = jax.random.randint(key_first, shape, 0, BLOCKS_DEV)
    second_pick = jax.random.randint(key_second, shape, 0, BLOCKS_DEV)
    low_pick = jnp.minimum(first_pick, second_pick)
    high_pick = jnp.maximum(first_pick, second_pick)
    rows_out = row_index * BLOCKS_DEV + jnp.where(remote, first_pick, low_pick)
    cols_out = owner_row * BLOCKS_DEV + jnp.where(remote, second_pick, high_pick)
    return (rows_out.reshape(N_ROWS, N_COLS * TILES_DEV).astype(jnp.int32), cols_out.reshape(N_ROWS, N_COLS * TILES_DEV).astype(jnp.int32))


def draw_block_rows(key, part):
    return block_pairs(key)[0]


def draw_block_cols(key, part):
    return block_pairs(key)[1]


def draw_counts(key, part):
    key = jax.random.fold_in(key, 2)
    row_index = jnp.arange(N_ROWS, dtype=jnp.int32)[:, None]
    reach = 1 + TILES_DEV * row_index // (2 * (N_ROWS - 1))
    cut_off = jax.random.randint(key, (N_ROWS, N_COLS), 0, 1 << 20) % reach
    return (TILES_DEV - cut_off).astype(jnp.int32)


def draw_start_vectors(key, part):
    key = jax.random.fold_in(key, 3)
    key_values = jax.random.fold_in(key, 1)
    key_columns = jax.random.fold_in(key, 2)
    cells = BLOCKS_DEV * BLOCK * N_ROWS
    row_place = (jnp.arange(cells) // (BLOCKS_DEV * BLOCK)).astype(jnp.float32) / (N_ROWS - 1)
    rising = 3.0 ** row_place
    column_scale = 2.0 ** jax.random.uniform(key_columns, (VECTORS,), jnp.float32)
    values = jnp.clip(jax.random.normal(key_values, (cells, VECTORS), jnp.float32), -9.0, 9.0)
    values = 1.0 + 0.08 * values
    return (values * rising[:, None] * column_scale[None, :]).astype(jnp.bfloat16)


def shard_levels(key, shape, shards, low, largest):
    level = 1.0
    for dim, parts in shards:
        draws = jax.random.uniform(jax.random.fold_in(jax.random.fold_in(key, 6), dim), (parts,), jnp.float32, low / len(shards), largest / len(shards))
        level = level * jnp.repeat(jnp.exp(draws), shape[dim] // parts).reshape((-1,) + (1,) * (len(shape) - 1 - dim))
    return level


def noise(own_key, shape, scale, limit, cuts=(), kind=jnp.bfloat16):
    array = scale * jax.random.normal(own_key, shape, jnp.float32)
    if cuts:
        array = array * shard_levels(own_key, shape, cuts, -0.22, 0.18)
    return jnp.clip(array, -limit, limit).astype(kind)


def setup_inputs(seed: int = 0, part: int = 0) -> dict:
    keys = jax.random.split(jax.random.key(seed), 7)
    part_keys = jax.random.split(jax.random.fold_in(keys[6], part), 7)
    return {
        "block_tiles": noise(part_keys[0], (N_ROWS, N_COLS * TILES_DEV, BLOCK, BLOCK), (2 * BLOCK * N_COLS * TILES_DEV // BLOCKS_DEV) ** -0.5, 0.0625, ((0, 4), (1, 4))),
        "block_rows": draw_block_rows(jax.random.fold_in(jax.random.fold_in(keys[6], part), 71), part),
        "block_cols": draw_block_cols(jax.random.fold_in(jax.random.fold_in(keys[6], part), 71), part),
        "counts": draw_counts(jax.random.fold_in(jax.random.fold_in(keys[6], part), 71), part),
        "cell_order": jax.vmap(lambda own: jax.random.permutation(own, CELLS_DEV))(jax.random.split(part_keys[4], N_ROWS)).reshape((N_ROWS, CELLS_DEV)).astype(jnp.int32),
        "start_vectors": draw_start_vectors(jax.random.fold_in(jax.random.fold_in(keys[6], part), 71), part),
    }


diag_shift = 3.0
tile_batch = 256
highest = lax.Precision.HIGHEST

def apply_blocks(flat_tiles, rows_flat, cols_flat, live_flat, vectors):
    blocks = vectors.reshape(-1, BLOCK, VECTORS)
    total_tiles = rows_flat.shape[0]
    group_size = math.gcd(total_tiles, tile_batch)
    group_count = total_tiles // group_size
    grouped = (flat_tiles.reshape(group_count, group_size, BLOCK, BLOCK), rows_flat.reshape(group_count, group_size), cols_flat.reshape(group_count, group_size), live_flat.reshape(group_count, group_size))

    def add_group(totals, pieces):
        tile_part, row_part, col_part, live_part = pieces
        matrices = tile_part.astype(jnp.float32)
        col_in = blocks[col_part].astype(jnp.float32)
        row_in = blocks[row_part].astype(jnp.float32)
        forward = jnp.einsum('tij,tjk->tik', matrices, col_in, precision=highest)
        backward = jnp.einsum('tji,tjk->tik', matrices, row_in, precision=highest).astype(jnp.bfloat16)
        backward = lax.optimization_barrier(backward).astype(jnp.float32)
        weight = live_part.astype(jnp.float32)[:, None, None]
        totals = totals.at[row_part].add(forward * weight)
        totals = totals.at[col_part].add(backward * weight)
        return (totals, None)
    totals, _ = lax.scan(add_group, jnp.zeros(blocks.shape, jnp.float32), grouped)
    return totals.reshape(-1, VECTORS)

def reference(block_tiles, block_rows, block_cols, counts, cell_order, start_vectors):
    cells_dev = cell_order.shape[1]
    offsets = (jnp.arange(N_ROWS, dtype=jnp.int32) * cells_dev)[:, None]
    vectors = start_vectors[(cell_order + offsets).reshape(-1)]
    position = jnp.arange(N_COLS * TILES_DEV, dtype=jnp.int32)
    live_tiles = (position[None, :] % TILES_DEV < counts[:, position // TILES_DEV]).astype(jnp.int32)
    flat_tiles = block_tiles.reshape(-1, BLOCK, BLOCK)
    total_cells = cells_dev * N_ROWS
    result = None
    for sweep_index in range(ITERS):
        applied = apply_blocks(flat_tiles, block_rows.reshape(-1), block_cols.reshape(-1), live_tiles.reshape(-1), vectors)
        applied = applied + diag_shift * vectors.astype(jnp.float32)
        gram_sum = jnp.dot(applied.T.astype(jnp.float32), applied.astype(jnp.float32), precision=highest, preferred_element_type=jnp.float32)
        lower_factor = jnp.linalg.cholesky(gram_sum / total_cells)
        identity = jnp.eye(VECTORS, dtype=jnp.float32)
        inverse = lax.linalg.triangular_solve(lower_factor, identity, left_side=True, lower=True)
        result = jnp.dot(applied.astype(jnp.float32), inverse.T.astype(jnp.float32), precision=highest, preferred_element_type=jnp.float32)
        vectors = result.astype(jnp.bfloat16)
    return result
```

```python
import functools

import jax
import jax.numpy as jnp
from jax import lax
from jax.experimental import pallas as pl
from jax.experimental.pallas import tpu as pltpu
from jax.sharding import PartitionSpec as P

ITERS = 2
MESH = pl.DeviceIdType.MESH
DIRECT = 16
diag_shift = 3.0
highest = lax.Precision.HIGHEST
f32 = jnp.float32
bf16 = jnp.bfloat16

F_TILE, F_IN, F_KEEP, G_TILE, G_IN, G_KEEP, F_LAST, G_LAST, R_TILE, R_ROW, WANT = range(11)


def route_kernel(row_count, blocks, rows_ref, cols_ref, counts_ref, tab_ref, want_ref, count, place):
    own_row = lax.axis_index("rows")
    tiles = rows_ref.shape[1]
    live_count = counts_ref[0, 0]

    def clear(i, _):
        for line in (R_TILE, WANT):
            tab_ref[line, i] = 0 if line == R_TILE else -1
        tab_ref[R_ROW, i] = -1
        return 0

    lax.fori_loop(0, row_count, clear, 0)
    for b in range(blocks + 1):
        count[0, b] = 0
        count[1, b] = 0

    def keys(t):
        col = cols_ref[0, t]
        owner = lax.div(col, blocks)
        a = rows_ref[0, t] - own_row * blocks
        b = col - owner * blocks
        live = t < live_count
        near = jnp.logical_and(live, owner == own_row)
        return a, b, owner, live, near

    def tally(t, _):
        a, b, owner, live, near = keys(t)
        ka = jnp.where(near, a, blocks)
        kb = jnp.where(near, b, blocks)
        count[0, ka] = count[0, ka] + 1
        count[1, kb] = count[1, kb] + 1

        @pl.when(jnp.logical_and(live, owner != own_row))
        def _():
            tab_ref[R_TILE, owner] = t
            tab_ref[R_ROW, owner] = a
            tab_ref[WANT, owner] = b

        return 0

    lax.fori_loop(0, tiles, tally, 0)
    for kind, last in ((0, F_LAST), (1, G_LAST)):
        total = jnp.int32(0)
        for b in range(blocks + 1):
            place[kind, b] = total
            here = count[kind, b]
            total = total + here
            if b < blocks:
                tab_ref[last, b] = jnp.where(here > 0, total, 0)
            count[kind, b] = 0

    def put(t, _):
        a, b, owner, live, near = keys(t)
        ka = jnp.where(near, a, blocks)
        kb = jnp.where(near, b, blocks)
        for kind, key, source, lines in (
            (0, ka, jnp.where(near, b, 0), (F_TILE, F_IN, F_KEEP)),
            (1, kb, jnp.where(near, a, 0), (G_TILE, G_IN, G_KEEP)),
        ):
            seen = count[kind, key]
            at = place[kind, key] + seen
            count[kind, key] = seen + 1
            tab_ref[lines[0], at] = t
            tab_ref[lines[1], at] = source
            tab_ref[lines[2], at] = jnp.minimum(seen, 1)
        return 0

    lax.fori_loop(0, tiles, put, 0)

    def wants(o, _):
        want_ref[o] = jnp.full(want_ref.shape[1:], tab_ref[WANT, o], jnp.int32)
        return 0

    lax.fori_loop(0, row_count, wants, 0)


def inverse_factor(gram):
    size = gram.shape[0]
    panels = size // 8
    lanes = lax.broadcasted_iota(jnp.int32, (8, size), 1)
    subs = lax.broadcasted_iota(jnp.int32, (8, size), 0)
    g = [gram[8 * r : 8 * r + 8, :] for r in range(panels)]
    w = [(lanes == subs + 8 * r).astype(f32) for r in range(panels)]
    done = []
    phase = 4

    def panel(_, carry):
        g, w = list(carry[0]), list(carry[1])
        n = len(g)
        col = [[jnp.broadcast_to(g[r][:, m : m + 1], (8, size)) for r in range(n)] for m in range(8)]
        pivots = jnp.ones((8, size), f32)
        for j in range(8):
            pivot = jnp.broadcast_to(col[j][0][j : j + 1, :], (8, size))
            pivots = jnp.where(subs == j, pivot, pivots)
            inv = 1.0 / pivot
            mult = [col[j][r] * inv for r in range(n)]
            mult[0] = jnp.where(subs > j, mult[0], 0.0)
            for m in range(j + 1, 8):
                row = jnp.broadcast_to(col[m][0][j : j + 1, :], (8, size))
                col[m] = [col[m][r] - mult[r] * row for r in range(n)]
            row = jnp.broadcast_to(g[0][j : j + 1, :], (8, size))
            g = [g[r] - mult[r] * row for r in range(n)]
            row = jnp.broadcast_to(w[0][j : j + 1, :], (8, size))
            w = [w[r] - mult[r] * row for r in range(n)]
        ready = w[0] * lax.rsqrt(pivots)
        g = [pltpu.roll(g[r], size - 8, 1) for r in range(1, n)] + [jnp.zeros((8, size), f32)]
        w = w[1:] + [ready]
        return tuple(g), tuple(w)

    while g:
        steps = min(phase, len(g))
        g, w = lax.fori_loop(0, steps, panel, (tuple(g), tuple(w)))
        g, w = list(g), list(w)
        keep = len(g) - steps
        done += w[keep:]
        g, w = g[:keep], w[:keep]
    return jnp.concatenate(done, axis=0)


def sweep_kernel(
    row_count, col_count, total_cells,
    tab_ref, want_ref, order_ref, start_ref, tiles_hbm, out_ref,
    tiles, near_f, near_g, vec, part, mid, app, answer, outgoing, fetched, returned, asked,
    half, cross, gram, pieces, whole, other,
    tile_sem, id_sems, ans_sems, ret_sems, half_sems, cross_sems, gat_sems, red_sems, all_sems, fly_sems,
):
    group = lax.axis_index("groups")
    row = lax.axis_index("rows")
    col = lax.axis_index("cols")
    blocks, width, block = vec.shape
    per = blocks // col_count
    tile_count = tiles.shape[0]
    low_rows = min(row_count, DIRECT // col_count)
    high_rows = row_count // low_rows
    members = low_rows * col_count
    strip = width // members
    near_col = col + 1 - 2 * lax.rem(col, 2)
    far_col = lax.rem(col + 2, 4)
    base_row = (row // low_rows) * low_rows
    own_id = (row - base_row) * col_count + col

    def every(first, last, body):
        if last - first <= 16:
            for d in range(first, last):
                body(d)
        else:
            lax.fori_loop(first, last, lambda d, c: (body(d), c)[1], 0)

    def member(e):
        q = lax.rem(own_id + e, members)
        return q, (group, base_row + q // col_count, lax.rem(q, col_count))

    def remote(src, dst, send, recv, device):
        return pltpu.make_async_remote_copy(
            src_ref=src, dst_ref=dst, send_sem=send, recv_sem=recv, device_id=device, device_id_type=MESH
        )

    load = pltpu.make_async_copy(tiles_hbm, tiles, tile_sem)
    load.start()

    barrier = pltpu.get_barrier_semaphore()

    def greet_row(d):
        pl.semaphore_signal(
            barrier, inc=1, device_id=(group, lax.rem(row + d, row_count), col), device_id_type=MESH
        )

    def greet_col(e):
        c = lax.rem(col + e, col_count)
        for r in range(low_rows):
            pl.semaphore_signal(barrier, inc=1, device_id=(group, base_row + r, c), device_id_type=MESH)

    every(1, row_count, greet_row)
    every(1, col_count, greet_col)
    pl.semaphore_wait(barrier, (row_count - 1) + (col_count - 1) * low_rows)

    def up(d):
        return (group, row + d, col)

    def down(d):
        return (group, row - d, col)

    def id_copy(d, device):
        return remote(want_ref.at[lax.rem(row + d, row_count)], asked.at[d], id_sems.at[0, d], id_sems.at[1, d], device)

    def send_ids(d):
        @pl.when(row + d < row_count)
        def _():
            id_copy(d, up(d)).start()

    every(1, row_count, send_ids)

    near_f[0] = jnp.zeros((width, block), f32)
    near_g[0] = jnp.zeros((width, block), f32)

    first = start_ref[...].astype(f32).T.astype(bf16)
    cells = first.shape[1]

    def permute(b, _):
        hit = lax.broadcasted_iota(jnp.int32, (cells, block), 0) == order_ref[b]
        vec[b] = jnp.dot(first, hit.astype(f32).astype(bf16), preferred_element_type=f32).astype(bf16)
        return 0

    lax.fori_loop(0, blocks, permute, 0)

    def finish_ids(d):
        @pl.when(row + d < row_count)
        def _():
            id_copy(d, up(d)).wait_send()

        @pl.when(row - d >= 0)
        def _():
            id_copy(d, up(d)).wait_recv()

    every(1, row_count, finish_ids)
    load.wait()

    for it in range(ITERS):

        def ans_copy(d):
            return remote(answer.at[it, d], fetched.at[it, d], ans_sems.at[it, 0, d], ans_sems.at[it, 1, d], down(d))

        def ret_copy(d):
            return remote(outgoing.at[it, d], returned.at[it, d], ret_sems.at[it, 0, d], ret_sems.at[it, 1, d], up(d))

        def send_far(d):
            @pl.when(row - d >= 0)
            def _():
                ids = asked[d][0:1, :]
                found = jnp.zeros((width, block), f32)
                for b in range(blocks):
                    found = jnp.where(ids == b, vec[b].astype(f32), found)
                answer[it, d] = found.astype(bf16)
                ans_copy(d).start()

            @pl.when(row + d < row_count)
            def _():
                peer = row + d
                a = jnp.maximum(tab_ref[R_ROW, peer], 0)
                outgoing[it, d] = jnp.dot(vec[a], tiles[tab_ref[R_TILE, peer]], preferred_element_type=f32).astype(bf16)
                ret_copy(d).start()

        every(1, row_count, send_far)

        def near(i, _):
            ahead = lax.dot_general(
                vec[tab_ref[F_IN, i]], tiles[tab_ref[F_TILE, i]], (((1,), (1,)), ((), ())), preferred_element_type=f32
            )
            near_f[i + 1] = near_f[i] * tab_ref[F_KEEP, i].astype(f32) + ahead
            back = jnp.dot(vec[tab_ref[G_IN, i]], tiles[tab_ref[G_TILE, i]], preferred_element_type=f32)
            near_g[i + 1] = near_g[i] * tab_ref[G_KEEP, i].astype(f32) + back.astype(bf16).astype(f32)
            return 0

        lax.fori_loop(0, tile_count, near, 0, unroll=2)
        for b in range(blocks):
            part[b // per, b % per] = near_f[tab_ref[F_LAST, b]] + near_g[tab_ref[G_LAST, b]]

        def take_far(d):
            @pl.when(row + d < row_count)
            def _():
                peer = row + d
                ret_copy(d).wait_send()
                ans_copy(d).wait_recv()
                ahead = lax.dot_general(
                    fetched[it, d], tiles[tab_ref[R_TILE, peer]], (((1,), (1,)), ((), ())), preferred_element_type=f32
                )
                a = tab_ref[R_ROW, peer]
                for b in range(blocks):
                    part[b // per, b % per] += ahead * (a == b).astype(f32)

            @pl.when(row - d >= 0)
            def _():
                ans_copy(d).wait_send()
                ret_copy(d).wait_recv()
                ids = asked[d][0:1, :]
                back = returned[it, d].astype(f32)
                for b in range(blocks):
                    part[b // per, b % per] += jnp.where(ids == b, back, 0.0)

        every(1, row_count, take_far)

        near_dev = (group, row, near_col)
        far_dev = (group, row, far_col)
        near_far = lax.rem(near_col + 2, 4)
        first_half = remote(part.at[near_far], half.at[it, 0], half_sems.at[it, 0, 0], half_sems.at[it, 1, 0], near_dev)
        second_half = remote(part.at[near_col], half.at[it, 1], half_sems.at[it, 0, 1], half_sems.at[it, 1, 1], near_dev)
        first_half.start()
        second_half.start()
        first_half.wait_recv()
        mid[...] = part[far_col] + half[it, 0]
        over = remote(mid, cross.at[it], cross_sems.at[it, 0], cross_sems.at[it, 1], far_dev)
        over.start()
        second_half.wait_recv()
        own = part[col] + half[it, 1]
        for k in range(per):
            app[it, col, k] = own[k] + diag_shift * vec[col * per + k].astype(f32)
        over.wait_recv()
        total = jnp.zeros((width, width), f32)
        for k in range(per):
            piece = app[it, col, k] + cross[it, k]
            app[it, col, k] = piece
            total = total + lax.dot_general(
                piece, piece, (((1,), (1,)), ((), ())), precision=highest, preferred_element_type=f32
            )
        gram[...] = total

        def red_copy(e):
            q, device = member(e)
            return remote(
                gram.at[pl.ds(pl.multiple_of(q * strip, strip), strip)],
                pieces.at[it, e], red_sems.at[it, 0, e], red_sems.at[it, 1, e], device,
            )

        mine = pl.ds(pl.multiple_of(own_id * strip, strip), strip)

        def all_copy(e):
            return remote(
                whole.at[it, mine], whole.at[it, mine], all_sems.at[it, 0, e], all_sems.at[it, 1, e], member(e)[1]
            )

        every(1, members, lambda e: red_copy(e).start())
        every(1, members, lambda e: red_copy(e).wait_recv())
        summed = gram[mine, :]
        for e in range(1, members):
            summed = summed + pieces[it, e]
        whole[it, mine] = summed
        every(1, members, lambda e: all_copy(e).start())
        every(1, members, lambda e: all_copy(e).wait_recv())
        every(1, members, lambda e: red_copy(e).wait_send())
        every(1, members, lambda e: all_copy(e).wait_send())
        gathered = whole[it]
        step = 0
        while (1 << step) < high_rows:
            span = low_rows << step
            peer = row + span - 2 * span * lax.rem(row // span, 2)
            other[it, step, 0] = gathered
            swap = remote(
                other.at[it, step, 0], other.at[it, step, 1],
                fly_sems.at[it, 0, step], fly_sems.at[it, 1, step], (group, peer, col),
            )
            swap.start()
            swap.wait()
            gathered = gathered + other[it, step, 1]
            step += 1

        last = it == ITERS - 1
        if not last:
            to_near = remote(app.at[it, col], app.at[it, col], gat_sems.at[0, 0], gat_sems.at[1, 0], near_dev)
            to_far = remote(app.at[it, col], app.at[it, col], gat_sems.at[0, 1], gat_sems.at[1, 1], far_dev)
            on = remote(app.at[it, far_col], app.at[it, far_col], gat_sems.at[0, 2], gat_sems.at[1, 2], near_dev)
            to_far.start()
            to_near.start()
        inverse = inverse_factor(gathered * (1.0 / total_cells))
        first_half.wait_send()
        second_half.wait_send()
        over.wait_send()
        if last:
            for k in range(per):
                res = jnp.dot(inverse, app[it, col, k], precision=highest, preferred_element_type=f32)
                out_ref[k * block : (k + 1) * block, :] = res.T
        else:
            to_far.wait_recv()
            on.start()
            to_near.wait_recv()
            on.wait_recv()
            to_far.wait_send()
            to_near.wait_send()
            on.wait_send()
            for b in range(blocks):
                vec[b] = jnp.dot(
                    inverse, app[it, b // per, b % per], precision=highest, preferred_element_type=f32
                ).astype(bf16)


def shards(block_tiles, block_rows, block_cols, counts, cell_order, start_vectors):
    row_count = lax.axis_size("rows")
    col_count = lax.axis_size("cols")
    stored = block_tiles.reshape(block_tiles.shape[1:])
    tile_count, block = stored.shape[0], stored.shape[1]
    cells = cell_order.shape[1]
    blocks = cells // block
    width = start_vectors.shape[1]
    per = blocks // col_count
    slots = max(row_count, tile_count, blocks)
    smem = pl.BlockSpec(memory_space=pltpu.SMEM)
    vmem = pl.BlockSpec(memory_space=pltpu.VMEM)
    table, wanted = pl.pallas_call(
        functools.partial(route_kernel, row_count, blocks),
        out_shape=(
            jax.ShapeDtypeStruct((11, slots), jnp.int32),
            jax.ShapeDtypeStruct((row_count, 8, block), jnp.int32),
        ),
        in_specs=[smem, smem, smem],
        out_specs=(smem, vmem),
        scratch_shapes=[pltpu.SMEM((2, blocks + 1), jnp.int32), pltpu.SMEM((2, blocks + 1), jnp.int32)],
    )(block_rows, block_cols, counts)
    members = min(row_count, DIRECT // col_count) * col_count
    strip = width // members
    fly = max(1, (row_count * col_count // members).bit_length() - 1)
    dma = pltpu.SemaphoreType.DMA
    return pl.pallas_call(
        functools.partial(sweep_kernel, row_count, col_count, cells * row_count),
        out_shape=jax.ShapeDtypeStruct((per * block, width), f32),
        in_specs=[smem, vmem, vmem, vmem, pl.BlockSpec(memory_space=pl.ANY)],
        out_specs=vmem,
        scratch_shapes=[
            pltpu.VMEM((tile_count, block, block), bf16),
            pltpu.VMEM((tile_count + 1, width, block), f32),
            pltpu.VMEM((tile_count + 1, width, block), f32),
            pltpu.VMEM((blocks, width, block), bf16),
            pltpu.VMEM((col_count, per, width, block), f32),
            pltpu.VMEM((per, width, block), f32),
            pltpu.VMEM((ITERS, col_count, per, width, block), f32),
            pltpu.VMEM((ITERS, row_count, width, block), bf16),
            pltpu.VMEM((ITERS, row_count, width, block), bf16),
            pltpu.VMEM((ITERS, row_count, width, block), bf16),
            pltpu.VMEM((ITERS, row_count, width, block), bf16),
            pltpu.VMEM((row_count, 8, block), jnp.int32),
            pltpu.VMEM((ITERS, 2, per, width, block), f32),
            pltpu.VMEM((ITERS, per, width, block), f32),
            pltpu.VMEM((width, width), f32),
            pltpu.VMEM((ITERS, members, strip, width), f32),
            pltpu.VMEM((ITERS, width, width), f32),
            pltpu.VMEM((ITERS, fly, 2, width, width), f32),
            dma,
            dma((2, row_count)),
            dma((ITERS, 2, row_count)),
            dma((ITERS, 2, row_count)),
            dma((ITERS, 2, 2)),
            dma((ITERS, 2)),
            dma((2, 3)),
            dma((ITERS, 2, members)),
            dma((ITERS, 2, members)),
            dma((ITERS, 2, fly)),
        ],
        compiler_params=pltpu.CompilerParams(
            collective_id=0, has_side_effects=True, vmem_limit_bytes=56 * 1024 * 1024
        ),
    )(table, wanted, cell_order.reshape(blocks, 1, block), start_vectors, stored)


def solution(mesh):
    in_specs = (
        P(("groups", "rows"), "cols", None, None),
        P(("groups", "rows"), "cols"),
        P(("groups", "rows"), "cols"),
        P(("groups", "rows"), "cols"),
        P(("groups", "rows"), None),
        P(("groups", "rows"), None),
    )
    out_specs = P(("groups", "rows", "cols"), None)
    return jax.shard_map(shards, mesh=mesh, in_specs=in_specs, out_specs=out_specs, check_vma=False)
```

```python
import functools

import jax
import jax.numpy as jnp
from jax import lax
from jax.experimental import pallas as pl
from jax.experimental.pallas import tpu as pltpu
from jax.sharding import PartitionSpec as P

ITERS = 2
MESH = pl.DeviceIdType.MESH
DIRECT = 4
diag_shift = 3.0
highest = lax.Precision.HIGHEST
f32 = jnp.float32
bf16 = jnp.bfloat16

F_TILE, F_IN, F_KEEP, G_TILE, G_IN, G_KEEP, F_LAST, G_LAST, R_TILE, R_ROW = range(10)


LINES = 16
LANES = 128


def route(row_count, blocks, own_row, rows_ref, cols_ref, counts_ref, lines_ref, want_ref):
    tiles = rows_ref.shape[1]
    i32 = jnp.int32
    square = (tiles, tiles)
    this = lax.broadcasted_iota(i32, square, 0)
    that = lax.broadcasted_iota(i32, square, 1)
    tile = lax.broadcasted_iota(i32, (tiles, LANES), 0)
    lane = lax.broadcasted_iota(i32, (tiles, LANES), 1)

    def count(flags, axis):
        return jnp.sum(jnp.where(flags, 1, 0), axis=axis, keepdims=True)

    def upright(line):
        return jnp.sum(jnp.where(this == that, jnp.broadcast_to(line, square), 0), axis=1, keepdims=True)

    def pick(flags, value):
        return jnp.sum(jnp.where(flags, value, 0), axis=0, keepdims=True)

    cols = cols_ref[...]
    owner = jnp.zeros(cols.shape, i32)
    for o in range(1, row_count):
        owner = owner + jnp.where(cols >= o * blocks, 1, 0)
    a = rows_ref[...] - own_row * blocks
    b = cols - owner * blocks
    live = jnp.where(lax.broadcasted_iota(i32, cols.shape, 1) < counts_ref[0, 0], 1, 0)
    local = jnp.where(owner == own_row, 1, 0)
    near = live * local
    for key, source, lines in ((a, b, (F_TILE, F_IN, F_KEEP, F_LAST)), (b, a, (G_TILE, G_IN, G_KEEP, G_LAST))):
        key = jnp.where(near > 0, key, blocks)
        own_key = upright(key)
        other = jnp.broadcast_to(key, square)
        equal = jnp.logical_and(other == own_key, that < this)
        seen = count(equal, 1)
        rank = count(other < own_key, 1) + seen
        here = rank == lane
        lines_ref[lines[0] : lines[0] + 1, :] = pick(here, tile)
        lines_ref[lines[1] : lines[1] + 1, :] = pick(here, upright(source * near))
        lines_ref[lines[2] : lines[2] + 1, :] = pick(here, jnp.minimum(seen, 1))
        lines_ref[lines[3] : lines[3] + 1, :] = jnp.where(count(own_key == lane, 0) > 0, count(own_key <= lane, 0), 0)
    far = jnp.logical_and(upright(owner) == lane, upright(live * (1 - local)) > 0)
    lines_ref[R_TILE : R_TILE + 1, :] = pick(far, tile)
    lines_ref[R_ROW : R_ROW + 1, :] = pick(far, upright(a) + 1) - 1
    want = pick(far, upright(b) + 1) - 1
    for o in range(row_count):
        want_ref[o] = jnp.broadcast_to(want[:, o : o + 1], want_ref.shape[1:])


def inverse_factor(gram):
    size = gram.shape[0]
    panels = size // 8
    lanes = lax.broadcasted_iota(jnp.int32, (8, size), 1)
    subs = lax.broadcasted_iota(jnp.int32, (8, size), 0)
    g = [gram[8 * r : 8 * r + 8, :] for r in range(panels)]
    w = [(lanes == subs + 8 * r).astype(f32) for r in range(panels)]
    done = []
    phase = 4

    def spread(x, j):
        return jnp.broadcast_to(x[j : j + 1, :], (8, size))

    def panel(i, carry):
        g, w = list(carry[0]), list(carry[1])
        n = len(g)
        p, q = jnp.where(lanes < size - 8 * i, g[0], 0.0), w[0]
        col = [jnp.broadcast_to(p[:, m : m + 1], (8, size)) for m in range(8)]
        pivots = jnp.ones((8, size), f32)
        for j in range(0, 8, 2):
            k = j + 1
            one, low, up, two = spread(col[j], j), spread(col[j], k), spread(col[k], j), spread(col[k], k)
            det = one * two - low * up
            inv = 1.0 / one
            inv_det = 1.0 / det
            step = low * inv
            pivots = jnp.where(subs == j, one, jnp.where(subs == k, det * inv, pivots))
            first = jnp.where(subs > j, col[j] * inv, 0.0)
            second = jnp.where(subs > k, (col[k] - first * up) * (one * inv_det), 0.0)

            def clear(x):
                top = spread(x, j)
                return x - first * top - second * (spread(x, k) - step * top)

            for m in range(j + 2, 8):
                col[m] = clear(col[m])
            p, q = clear(p), clear(q)
        factors = jnp.transpose(p / pivots)
        p_rows = [spread(p, j) for j in range(8)]
        q_rows = [spread(q, j) for j in range(8)]
        for r in range(1, n):
            for j in range(8):
                mult = jnp.broadcast_to(factors[8 * r : 8 * r + 8, j : j + 1], (8, size))
                g[r] = g[r] - mult * p_rows[j]
                w[r] = w[r] - mult * q_rows[j]
        g = [pltpu.roll(g[r], size - 8, 1) for r in range(1, n)] + [jnp.zeros((8, size), f32)]
        w = w[1:] + [q * lax.rsqrt(pivots)]
        return tuple(g), tuple(w)

    at = 0
    while g:
        steps = min(phase, len(g))
        g, w = lax.fori_loop(at, at + steps, panel, (tuple(g), tuple(w)))
        g, w = list(g), list(w)
        at += steps
        keep = len(g) - steps
        done += w[keep:]
        g, w = g[:keep], w[:keep]
    return jnp.concatenate(done, axis=0)


def sweep_kernel(
    row_count, col_count, total_cells,
    rows_ref, cols_ref, counts_ref, order_ref, start_ref, tiles_hbm, out_ref, inverse_ref,
    lines_ref, tab_ref, want_ref,
    tiles, near_f, near_g, vec, part, mid, app, answer, outgoing, fetched, returned, asked,
    half, cross, part16, mid16, half16, cross16, gram, pieces, strips, whole, other,
    tile_sem, tab_sem, id_sems, ans_sems, ret_sems, half_sems, cross_sems, gat_sems, red_sems, row_sems, all_sems, fly_sems,
):
    group = lax.axis_index("groups")
    row = lax.axis_index("rows")
    col = lax.axis_index("cols")
    blocks, width, block = vec.shape
    per = blocks // col_count
    tile_count = tiles.shape[0]
    low_rows = min(row_count, DIRECT)
    high_rows = row_count // low_rows
    strip = width // col_count
    near_col = col + 1 - 2 * lax.rem(col, 2)
    far_col = lax.rem(col + 2, 4)
    base_row = (row // low_rows) * low_rows
    low_row = row - base_row

    def every(first, last, body):
        if last - first <= 16:
            for d in range(first, last):
                body(d)
        else:
            lax.fori_loop(first, last, lambda d, c: (body(d), c)[1], 0)

    def remote(src, dst, send, recv, device):
        return pltpu.make_async_remote_copy(
            src_ref=src, dst_ref=dst, send_sem=send, recv_sem=recv, device_id=device, device_id_type=MESH
        )

    load = pltpu.make_async_copy(tiles_hbm, tiles, tile_sem)
    load.start()

    barrier = pltpu.get_barrier_semaphore()

    def greet_row(d):
        pl.semaphore_signal(
            barrier, inc=1, device_id=(group, lax.rem(row + d, row_count), col), device_id_type=MESH
        )

    def greet_col(e):
        pl.semaphore_signal(
            barrier, inc=1, device_id=(group, row, lax.rem(col + e, col_count)), device_id_type=MESH
        )

    every(1, row_count, greet_row)
    every(1, col_count, greet_col)
    route(row_count, blocks, row, rows_ref, cols_ref, counts_ref, lines_ref, want_ref)
    table = pltpu.make_async_copy(lines_ref, tab_ref, tab_sem)
    table.start()
    pl.semaphore_wait(barrier, (row_count - 1) + (col_count - 1))

    def up(d):
        return (group, row + d, col)

    def down(d):
        return (group, row - d, col)

    def id_copy(d, device):
        return remote(want_ref.at[lax.rem(row + d, row_count)], asked.at[d], id_sems.at[0, d], id_sems.at[1, d], device)

    def send_ids(d):
        @pl.when(row + d < row_count)
        def _():
            id_copy(d, up(d)).start()

    every(1, row_count, send_ids)

    near_f[0] = jnp.zeros((width, block), f32)
    near_g[0] = jnp.zeros((width, block), f32)

    first = start_ref[...].astype(f32).T.astype(bf16)
    cells = first.shape[1]

    def permute(b, _):
        hit = lax.broadcasted_iota(jnp.int32, (cells, block), 0) == order_ref[b]
        vec[b] = jnp.dot(first, hit.astype(f32).astype(bf16), preferred_element_type=f32).astype(bf16)
        return 0

    lax.fori_loop(0, blocks, permute, 0)

    def finish_ids(d):
        @pl.when(row + d < row_count)
        def _():
            id_copy(d, up(d)).wait_send()

        @pl.when(row - d >= 0)
        def _():
            id_copy(d, up(d)).wait_recv()

    every(1, row_count, finish_ids)
    table.wait()
    load.wait()

    for it in range(ITERS):

        def ans_copy(d):
            return remote(answer.at[it, d], fetched.at[it, d], ans_sems.at[it, 0, d], ans_sems.at[it, 1, d], down(d))

        def ret_copy(d):
            return remote(outgoing.at[it, d], returned.at[it, d], ret_sems.at[it, 0, d], ret_sems.at[it, 1, d], up(d))

        def send_far(d):
            @pl.when(row - d >= 0)
            def _():
                ids = asked[d][0:1, :]
                found = jnp.zeros((width, block), f32)
                for b in range(blocks):
                    found = jnp.where(ids == b, vec[b].astype(f32), found)
                answer[it, d] = found.astype(bf16)
                ans_copy(d).start()

            @pl.when(row + d < row_count)
            def _():
                peer = row + d
                a = jnp.maximum(tab_ref[R_ROW, peer], 0)
                outgoing[it, d] = jnp.dot(vec[a], tiles[tab_ref[R_TILE, peer]], preferred_element_type=f32).astype(bf16)
                ret_copy(d).start()

        every(1, row_count, send_far)

        def near(i, _):
            ahead = lax.dot_general(
                vec[tab_ref[F_IN, i]], tiles[tab_ref[F_TILE, i]], (((1,), (1,)), ((), ())), preferred_element_type=f32
            )
            near_f[i + 1] = near_f[i] * tab_ref[F_KEEP, i].astype(f32) + ahead
            back = jnp.dot(vec[tab_ref[G_IN, i]], tiles[tab_ref[G_TILE, i]], preferred_element_type=f32)
            near_g[i + 1] = near_g[i] * tab_ref[G_KEEP, i].astype(f32) + back.astype(bf16).astype(f32)
            return 0

        lax.fori_loop(0, tile_count, near, 0, unroll=2)
        for b in range(blocks):
            part[b // per, b % per] = near_f[tab_ref[F_LAST, b]] + near_g[tab_ref[G_LAST, b]]

        def take_far(d):
            @pl.when(row + d < row_count)
            def _():
                peer = row + d
                ret_copy(d).wait_send()
                ans_copy(d).wait_recv()
                ahead = lax.dot_general(
                    fetched[it, d], tiles[tab_ref[R_TILE, peer]], (((1,), (1,)), ((), ())), preferred_element_type=f32
                )
                a = tab_ref[R_ROW, peer]
                for b in range(blocks):
                    part[b // per, b % per] += ahead * (a == b).astype(f32)

            @pl.when(row - d >= 0)
            def _():
                ans_copy(d).wait_send()
                ret_copy(d).wait_recv()
                ids = asked[d][0:1, :]
                back = returned[it, d].astype(f32)
                for b in range(blocks):
                    part[b // per, b % per] += jnp.where(ids == b, back, 0.0)

        every(1, row_count, take_far)

        last = it == ITERS - 1
        near_dev = (group, row, near_col)
        far_dev = (group, row, far_col)
        near_far = lax.rem(near_col + 2, 4)
        if last:
            part16[near_far] = part[near_far].astype(bf16)
            part16[near_col] = part[near_col].astype(bf16)
        out, arrived, sent, crossed = (part16, half16, mid16, cross16) if last else (part, half, mid, cross)
        first_half = remote(out.at[near_far], arrived.at[0], half_sems.at[it, 0, 0], half_sems.at[it, 1, 0], near_dev)
        second_half = remote(out.at[near_col], arrived.at[1], half_sems.at[it, 0, 1], half_sems.at[it, 1, 1], near_dev)
        first_half.start()
        second_half.start()
        first_half.wait_recv()
        sent[...] = (part[far_col] + arrived[0].astype(f32)).astype(sent.dtype)
        over = remote(sent, crossed, cross_sems.at[it, 0], cross_sems.at[it, 1], far_dev)
        over.start()
        second_half.wait_recv()
        own = part[col] + arrived[1].astype(f32)
        for k in range(per):
            part[col, k] = own[k] + diag_shift * vec[col * per + k].astype(f32)
        over.wait_recv()
        for k in range(per):
            piece = part[col, k] + crossed[k].astype(f32)
            if last:
                out_ref[k] = piece
            else:
                app[col, k] = piece

        def gat_copy(kind, k, quarter, device):
            place = app.at[quarter, k]
            return remote(place, place, gat_sems.at[0, kind, k], gat_sems.at[1, kind, k], device)

        to_far = [gat_copy(0, k, col, far_dev) for k in range(per)]
        to_near = [gat_copy(1, k, col, near_dev) for k in range(per)]
        onward = [gat_copy(2, k, far_col, near_dev) for k in range(per)]
        total = jnp.zeros((width, width), f32)
        for k in range(per):
            piece = out_ref[k] if last else app[col, k]
            total = total + lax.dot_general(
                piece, piece, (((1,), (1,)), ((), ())), precision=highest, preferred_element_type=f32
            )
        gram[...] = total

        def peer_col(e):
            return (group, row, lax.rem(col + e, col_count))

        def red_copy(e):
            q = lax.rem(col + e, col_count)
            return remote(
                gram.at[pl.ds(pl.multiple_of(q * strip, strip), strip)],
                pieces.at[it, e], red_sems.at[it, 0, e], red_sems.at[it, 1, e], peer_col(e),
            )

        def row_copy(d):
            place = strips.at[it, low_row]
            device = (group, base_row + lax.rem(low_row + d, low_rows), col)
            return remote(place, place, row_sems.at[it, 0, d], row_sems.at[it, 1, d], device)

        mine = pl.ds(pl.multiple_of(col * strip, strip), strip)

        def all_copy(e):
            place = whole.at[it, mine]
            return remote(place, place, all_sems.at[it, 0, e], all_sems.at[it, 1, e], peer_col(e))

        every(1, col_count, lambda e: red_copy(e).start())
        every(1, col_count, lambda e: red_copy(e).wait_recv())
        summed = gram[mine, :]
        for e in range(1, col_count):
            summed = summed + pieces[it, e]
        strips[it, low_row] = summed
        every(1, low_rows, lambda d: row_copy(d).start())
        every(1, low_rows, lambda d: row_copy(d).wait_recv())
        summed = strips[it, 0]
        for d in range(1, low_rows):
            summed = summed + strips[it, d]
        step = 0
        while (1 << step) < high_rows:
            span = low_rows << step
            peer = row + span - 2 * span * lax.rem(row // span, 2)
            other[it, step, 0] = summed
            swap = remote(
                other.at[it, step, 0], other.at[it, step, 1],
                fly_sems.at[it, 0, step], fly_sems.at[it, 1, step], (group, peer, col),
            )
            swap.start()
            swap.wait()
            summed = summed + other[it, step, 1]
            step += 1
        whole[it, mine] = summed
        every(1, col_count, lambda e: all_copy(e).start())
        every(1, col_count, lambda e: all_copy(e).wait_recv())
        if not last:
            for k in range(per):
                to_far[k].start()
                to_near[k].start()
        if not last:
            for k in range(per):
                pass
        inverse = inverse_factor(whole[it] * (1.0 / total_cells))
        every(1, col_count, lambda e: red_copy(e).wait_send())
        every(1, low_rows, lambda d: row_copy(d).wait_send())
        every(1, col_count, lambda e: all_copy(e).wait_send())
        first_half.wait_send()
        second_half.wait_send()
        over.wait_send()
        if last:
            inverse_ref[...] = inverse
        else:
            for k in range(per):
                to_far[k].wait_recv()
                onward[k].start()
            for k in range(per):
                to_near[k].wait_recv()
                onward[k].wait_recv()
                to_far[k].wait_send()
                to_near[k].wait_send()
                onward[k].wait_send()
            for b in range(blocks):
                vec[b] = jnp.dot(
                    inverse, app[b // per, b % per], precision=highest, preferred_element_type=f32
                ).astype(bf16)


def shards(block_tiles, block_rows, block_cols, counts, cell_order, start_vectors):
    row_count = lax.axis_size("rows")
    col_count = lax.axis_size("cols")
    stored = block_tiles.reshape(block_tiles.shape[1:])
    tile_count, block = stored.shape[0], stored.shape[1]
    cells = cell_order.shape[1]
    blocks = cells // block
    width = start_vectors.shape[1]
    per = blocks // col_count
    smem = pl.BlockSpec(memory_space=pltpu.SMEM)
    vmem = pl.BlockSpec(memory_space=pltpu.VMEM)
    low_rows = min(row_count, DIRECT)
    strip = width // col_count
    fly = max(1, (row_count // low_rows).bit_length() - 1)
    dma = pltpu.SemaphoreType.DMA
    applied, inverse = pl.pallas_call(
        functools.partial(sweep_kernel, row_count, col_count, cells * row_count),
        out_shape=(jax.ShapeDtypeStruct((per, width, block), f32), jax.ShapeDtypeStruct((width, width), f32)),
        in_specs=[vmem, vmem, smem, vmem, vmem, pl.BlockSpec(memory_space=pl.ANY)],
        out_specs=(vmem, vmem),
        scratch_shapes=[
            pltpu.VMEM((LINES, LANES), jnp.int32),
            pltpu.SMEM((LINES, LANES), jnp.int32),
            pltpu.VMEM((row_count, 8, block), jnp.int32),
            pltpu.VMEM((tile_count, block, block), bf16),
            pltpu.VMEM((tile_count + 1, width, block), f32),
            pltpu.VMEM((tile_count + 1, width, block), f32),
            pltpu.VMEM((blocks, width, block), bf16),
            pltpu.VMEM((col_count, per, width, block), f32),
            pltpu.VMEM((per, width, block), f32),
            pltpu.VMEM((col_count, per, width, block), f32),
            pltpu.VMEM((ITERS, row_count, width, block), bf16),
            pltpu.VMEM((ITERS, row_count, width, block), bf16),
            pltpu.VMEM((ITERS, row_count, width, block), bf16),
            pltpu.VMEM((ITERS, row_count, width, block), bf16),
            pltpu.VMEM((row_count, 8, block), jnp.int32),
            pltpu.VMEM((2, per, width, block), f32),
            pltpu.VMEM((per, width, block), f32),
            pltpu.VMEM((col_count, per, width, block), bf16),
            pltpu.VMEM((per, width, block), bf16),
            pltpu.VMEM((2, per, width, block), bf16),
            pltpu.VMEM((per, width, block), bf16),
            pltpu.VMEM((width, width), f32),
            pltpu.VMEM((ITERS, col_count, strip, width), f32),
            pltpu.VMEM((ITERS, low_rows, strip, width), f32),
            pltpu.VMEM((ITERS, width, width), f32),
            pltpu.VMEM((ITERS, fly, 2, strip, width), f32),
            dma,
            dma,
            dma((2, row_count)),
            dma((ITERS, 2, row_count)),
            dma((ITERS, 2, row_count)),
            dma((ITERS, 2, 2)),
            dma((ITERS, 2)),
            dma((2, 3, per)),
            dma((ITERS, 2, col_count)),
            dma((ITERS, 2, low_rows)),
            dma((ITERS, 2, col_count)),
            dma((ITERS, 2, fly)),
        ],
        compiler_params=pltpu.CompilerParams(
            collective_id=0, has_side_effects=True, vmem_limit_bytes=56 * 1024 * 1024
        ),
    )(block_rows, block_cols, counts, cell_order.reshape(blocks, 1, block), start_vectors, stored)
    result = jnp.einsum("kwb,vw->kbv", applied, inverse, precision=highest, preferred_element_type=f32)
    return result.reshape(per * block, width)


def solution(mesh):
    in_specs = (
        P(("groups", "rows"), "cols", None, None),
        P(("groups", "rows"), "cols"),
        P(("groups", "rows"), "cols"),
        P(("groups", "rows"), "cols"),
        P(("groups", "rows"), None),
        P(("groups", "rows"), None),
    )
    out_specs = P(("groups", "rows", "cols"), None)
    return jax.shard_map(shards, mesh=mesh, in_specs=in_specs, out_specs=out_specs, check_vma=False)
```

```python
import functools

import jax
import jax.numpy as jnp
from jax import lax
from jax.experimental import pallas as pl
from jax.experimental.pallas import tpu as pltpu
from jax.sharding import PartitionSpec as P

ITERS = 2
MESH = pl.DeviceIdType.MESH
DIRECT = 4
diag_shift = 3.0
highest = lax.Precision.HIGHEST
f32 = jnp.float32
bf16 = jnp.bfloat16

F_TILE, F_IN, F_KEEP, G_TILE, G_IN, G_KEEP, F_LAST, G_LAST, R_TILE, R_ROW = range(10)


LINES = 16
LANES = 128


def route(row_count, blocks, own_row, rows_ref, cols_ref, counts_ref, lines_ref, want_ref):
    tiles = rows_ref.shape[1]
    i32 = jnp.int32
    square = (tiles, tiles)
    this = lax.broadcasted_iota(i32, square, 0)
    that = lax.broadcasted_iota(i32, square, 1)
    tile = lax.broadcasted_iota(i32, (tiles, LANES), 0)
    lane = lax.broadcasted_iota(i32, (tiles, LANES), 1)

    def count(flags, axis):
        return jnp.sum(jnp.where(flags, 1, 0), axis=axis, keepdims=True)

    def upright(line):
        return jnp.sum(jnp.where(this == that, jnp.broadcast_to(line, square), 0), axis=1, keepdims=True)

    def pick(flags, value):
        return jnp.sum(jnp.where(flags, value, 0), axis=0, keepdims=True)

    cols = cols_ref[...]
    owner = jnp.zeros(cols.shape, i32)
    for o in range(1, row_count):
        owner = owner + jnp.where(cols >= o * blocks, 1, 0)
    a = rows_ref[...] - own_row * blocks
    b = cols - owner * blocks
    live = jnp.where(lax.broadcasted_iota(i32, cols.shape, 1) < counts_ref[0, 0], 1, 0)
    local = jnp.where(owner == own_row, 1, 0)
    near = live * local
    for key, source, lines in ((a, b, (F_TILE, F_IN, F_KEEP, F_LAST)), (b, a, (G_TILE, G_IN, G_KEEP, G_LAST))):
        key = jnp.where(near > 0, key, blocks)
        own_key = upright(key)
        other = jnp.broadcast_to(key, square)
        equal = jnp.logical_and(other == own_key, that < this)
        seen = count(equal, 1)
        rank = count(other < own_key, 1) + seen
        here = rank == lane
        lines_ref[lines[0] : lines[0] + 1, :] = pick(here, tile)
        lines_ref[lines[1] : lines[1] + 1, :] = pick(here, upright(source * near))
        lines_ref[lines[2] : lines[2] + 1, :] = pick(here, jnp.minimum(seen, 1))
        lines_ref[lines[3] : lines[3] + 1, :] = jnp.where(count(own_key == lane, 0) > 0, count(own_key <= lane, 0), 0)
    far = jnp.logical_and(upright(owner) == lane, upright(live * (1 - local)) > 0)
    lines_ref[R_TILE : R_TILE + 1, :] = pick(far, tile)
    lines_ref[R_ROW : R_ROW + 1, :] = pick(far, upright(a) + 1) - 1
    want = pick(far, upright(b) + 1) - 1
    for o in range(row_count):
        want_ref[o] = jnp.broadcast_to(want[:, o : o + 1], want_ref.shape[1:])


def inverse_factor(gram, aside):
    size = gram.shape[0]
    panels = size // 8
    lanes = lax.broadcasted_iota(jnp.int32, (8, size), 1)
    subs = lax.broadcasted_iota(jnp.int32, (8, size), 0)
    g = [gram[8 * r : 8 * r + 8, :] for r in range(panels)]
    w = [(lanes == subs + 8 * r).astype(f32) for r in range(panels)]
    done = []
    phase = 4

    def spread(x, j):
        return jnp.broadcast_to(x[j : j + 1, :], (8, size))

    def panel(i, carry):
        g, w = list(carry[0]), list(carry[1])
        n = len(g)
        p, q = jnp.where(lanes < size - 8 * i, g[0], 0.0), w[0]
        col = [jnp.broadcast_to(p[:, m : m + 1], (8, size)) for m in range(8)]
        pivots = jnp.ones((8, size), f32)
        for j in range(0, 8, 2):
            k = j + 1
            one, low, up, two = spread(col[j], j), spread(col[j], k), spread(col[k], j), spread(col[k], k)
            det = one * two - low * up
            inv = 1.0 / one
            inv_det = 1.0 / det
            step = low * inv
            pivots = jnp.where(subs == j, one, jnp.where(subs == k, det * inv, pivots))
            first = jnp.where(subs > j, col[j] * inv, 0.0)
            second = jnp.where(subs > k, (col[k] - first * up) * (one * inv_det), 0.0)

            def clear(x):
                top = spread(x, j)
                return x - first * top - second * (spread(x, k) - step * top)

            for m in range(j + 2, 8):
                col[m] = clear(col[m])
            p, q = clear(p), clear(q)
        factors = jnp.transpose(p / pivots)
        p_rows = [spread(p, j) for j in range(8)]
        q_rows = [spread(q, j) for j in range(8)]
        for r in range(1, n):
            for j in range(8):
                mult = jnp.broadcast_to(factors[8 * r : 8 * r + 8, j : j + 1], (8, size))
                g[r] = g[r] - mult * p_rows[j]
                w[r] = w[r] - mult * q_rows[j]
        g = [pltpu.roll(g[r], size - 8, 1) for r in range(1, n)] + [jnp.zeros((8, size), f32)]
        w = w[1:] + [q * lax.rsqrt(pivots)]
        return tuple(g), tuple(w)

    at = 0
    while g:
        steps = min(phase, len(g))
        g, w = lax.fori_loop(at, at + steps, panel, (tuple(g), tuple(w)))
        g, w = list(g), list(w)
        at += steps
        if len(g) == 2 * phase:
            aside()
        keep = len(g) - steps
        done += w[keep:]
        g, w = g[:keep], w[:keep]
    return jnp.concatenate(done, axis=0)


def sweep_kernel(
    row_count, col_count, total_cells,
    rows_ref, cols_ref, counts_ref, order_ref, start_ref, tiles_hbm, out_ref, inverse_ref,
    lines_ref, tab_ref, want_ref,
    tiles, near_f, near_g, vec, part, app, answer, outgoing, fetched, returned, asked,
    half, part16, mid16, half16, cross16, gram, pieces, strips, whole, other, common, share, shared,
    tile_sem, tab_sem, share_sems, id_sems, ans_sems, ret_sems, half_sems, cross_sems, gat_sems, red_sems, row_sems, all_sems, fly_sems,
):
    group = lax.axis_index("groups")
    row = lax.axis_index("rows")
    col = lax.axis_index("cols")
    blocks, width, block = vec.shape
    per = blocks // col_count
    tile_count = tiles.shape[0]
    low_rows = min(row_count, DIRECT)
    high_rows = row_count // low_rows
    strip = width // col_count
    near_col = col + 1 - 2 * lax.rem(col, 2)
    far_col = lax.rem(col + 2, 4)
    base_row = (row // low_rows) * low_rows
    low_row = row - base_row

    def every(first, last, body):
        if last - first <= 16:
            for d in range(first, last):
                body(d)
        else:
            lax.fori_loop(first, last, lambda d, c: (body(d), c)[1], 0)

    def remote(src, dst, send, recv, device):
        return pltpu.make_async_remote_copy(
            src_ref=src, dst_ref=dst, send_sem=send, recv_sem=recv, device_id=device, device_id_type=MESH
        )

    load = pltpu.make_async_copy(tiles_hbm, tiles, tile_sem)
    load.start()

    barrier = pltpu.get_barrier_semaphore()

    def greet_row(d):
        pl.semaphore_signal(
            barrier, inc=1, device_id=(group, lax.rem(row + d, row_count), col), device_id_type=MESH
        )

    def greet_col(e):
        pl.semaphore_signal(
            barrier, inc=1, device_id=(group, row, lax.rem(col + e, col_count)), device_id_type=MESH
        )

    every(1, row_count, greet_row)
    every(1, col_count, greet_col)
    route(row_count, blocks, row, rows_ref, cols_ref, counts_ref, lines_ref, want_ref)
    table = pltpu.make_async_copy(lines_ref, tab_ref, tab_sem)
    table.start()
    first = start_ref[...].astype(f32).T.astype(bf16)
    cells = first.shape[1]

    def permute(b, _):
        hit = lax.broadcasted_iota(jnp.int32, (cells, block), 0) == order_ref[b]
        vec[b] = jnp.dot(first, hit.astype(f32).astype(bf16), preferred_element_type=f32).astype(bf16)
        return 0

    lax.fori_loop(0, blocks, permute, 0)
    mean = vec[0].astype(f32)
    for b in range(1, blocks):
        mean = mean + vec[b].astype(f32)
    mean = jnp.sum(mean, axis=1, keepdims=True) * (1.0 / cells)
    scale = lax.rsqrt(jnp.maximum(jnp.sum(mean * mean, axis=0, keepdims=True), 1e-30))
    common[...] = jnp.broadcast_to(mean * scale, common.shape)

    pl.semaphore_wait(barrier, (row_count - 1) + (col_count - 1))

    def up(d):
        return (group, row + d, col)

    def down(d):
        return (group, row - d, col)

    def id_copy(d, device):
        return remote(want_ref.at[lax.rem(row + d, row_count)], asked.at[d], id_sems.at[0, d], id_sems.at[1, d], device)

    def send_ids(d):
        @pl.when(row + d < row_count)
        def _():
            id_copy(d, up(d)).start()

    every(1, row_count, send_ids)

    near_f[0] = jnp.zeros((width, block), f32)
    near_g[0] = jnp.zeros((width, block), f32)

    def finish_ids(d):
        @pl.when(row + d < row_count)
        def _():
            id_copy(d, up(d)).wait_send()

        @pl.when(row - d >= 0)
        def _():
            id_copy(d, up(d)).wait_recv()

    table.wait()
    load.wait()

    for it in range(ITERS):

        def ans_copy(d):
            return remote(answer.at[it, d], fetched.at[it, d], ans_sems.at[it, 0, d], ans_sems.at[it, 1, d], down(d))

        def ret_copy(d):
            return remote(outgoing.at[it, d], returned.at[it, d], ret_sems.at[it, 0, d], ret_sems.at[it, 1, d], up(d))

        def send_down(d):
            @pl.when(row - d >= 0)
            def _():
                ids = asked[d][0:1, :]
                found = jnp.zeros((width, block), f32)
                for b in range(blocks):
                    found = jnp.where(ids == b, vec[b].astype(f32), found)
                answer[it, d] = found.astype(bf16)
                ans_copy(d).start()

        def send_up(d):
            @pl.when(row + d < row_count)
            def _():
                peer = row + d
                a = jnp.maximum(tab_ref[R_ROW, peer], 0)
                outgoing[it, d] = jnp.dot(vec[a], tiles[tab_ref[R_TILE, peer]], preferred_element_type=f32).astype(bf16)
                ret_copy(d).start()

        every(1, row_count, send_up)
        if it > 0:
            every(1, row_count, send_down)

        def near(i, _):
            ahead = lax.dot_general(
                vec[tab_ref[F_IN, i]], tiles[tab_ref[F_TILE, i]], (((1,), (1,)), ((), ())), preferred_element_type=f32
            )
            near_f[i + 1] = near_f[i] * tab_ref[F_KEEP, i].astype(f32) + ahead
            back = jnp.dot(vec[tab_ref[G_IN, i]], tiles[tab_ref[G_TILE, i]], preferred_element_type=f32)
            near_g[i + 1] = near_g[i] * tab_ref[G_KEEP, i].astype(f32) + back.astype(bf16).astype(f32)
            return 0

        early = tile_count // 4 if it == 0 else 0
        if it == 0:
            lax.fori_loop(0, early, near, 0, unroll=2)
            every(1, row_count, finish_ids)
            every(1, row_count, send_down)
        lax.fori_loop(early, tile_count, near, 0, unroll=2)
        for b in range(blocks):
            part[b // per, b % per] = near_f[tab_ref[F_LAST, b]] + near_g[tab_ref[G_LAST, b]]

        def take_far(d):
            @pl.when(row + d < row_count)
            def _():
                peer = row + d
                ret_copy(d).wait_send()
                ans_copy(d).wait_recv()
                ahead = lax.dot_general(
                    fetched[it, d], tiles[tab_ref[R_TILE, peer]], (((1,), (1,)), ((), ())), preferred_element_type=f32
                )
                a = tab_ref[R_ROW, peer]
                for b in range(blocks):
                    part[b // per, b % per] += ahead * (a == b).astype(f32)

            @pl.when(row - d >= 0)
            def _():
                ans_copy(d).wait_send()
                ret_copy(d).wait_recv()
                ids = asked[d][0:1, :]
                back = returned[it, d].astype(f32)
                for b in range(blocks):
                    part[b // per, b % per] += jnp.where(ids == b, back, 0.0)

        every(1, row_count, take_far)

        last = it == ITERS - 1
        near_dev = (group, row, near_col)
        far_dev = (group, row, far_col)
        near_far = lax.rem(near_col + 2, 4)
        if last:
            part16[near_far] = part[near_far].astype(bf16)
            part16[near_col] = part[near_col].astype(bf16)
        out, arrived = (part16, half16) if last else (part, half)
        sent, crossed = mid16.at[it], cross16.at[it]
        shares = remote(share, shared, share_sems.at[0], share_sems.at[1], far_dev)
        first_half = remote(out.at[near_far], arrived.at[0], half_sems.at[it, 0, 0], half_sems.at[it, 1, 0], near_dev)
        second_half = remote(out.at[near_col], arrived.at[1], half_sems.at[it, 0, 1], half_sems.at[it, 1, 1], near_dev)
        first_half.start()
        second_half.start()
        first_half.wait_recv()
        for k in range(per):
            value = part[far_col, k] + arrived[0, k].astype(f32)
            if not last:
                along = jnp.sum(common[...] * value, axis=0, keepdims=True)
                share[k] = jnp.broadcast_to(along, share.shape[1:])
                value = value - common[...] * along
            sent[k] = value.astype(bf16)
        if not last:
            shares.start()
        over = remote(sent, crossed, cross_sems.at[it, 0], cross_sems.at[it, 1], far_dev)
        over.start()
        second_half.wait_recv()
        own = part[col] + arrived[1].astype(f32)
        for k in range(per):
            part[col, k] = own[k] + diag_shift * vec[col * per + k].astype(f32)
        if not last:
            shares.wait_recv()
        over.wait_recv()
        for k in range(per):
            piece = part[col, k] + crossed[k].astype(f32)
            if not last:
                piece = piece + common[...] * shared[k, 0:1, :]
            app[it, col, k] = piece

        def gat_copy(kind, k, quarter, device):
            place = app.at[it, quarter, k]
            return remote(place, place, gat_sems.at[0, kind, k], gat_sems.at[1, kind, k], device)

        to_far = [gat_copy(0, k, col, far_dev) for k in range(per)]
        to_near = [gat_copy(1, k, col, near_dev) for k in range(per)]
        onward = [gat_copy(2, k, far_col, near_dev) for k in range(per)]
        total = jnp.zeros((width, width), f32)
        for k in range(per):
            piece = app[it, col, k]
            total = total + lax.dot_general(
                piece, piece, (((1,), (1,)), ((), ())), precision=highest, preferred_element_type=f32
            )
        gram[...] = total

        def peer_col(e):
            return (group, row, lax.rem(col + e, col_count))

        def red_copy(e):
            q = lax.rem(col + e, col_count)
            return remote(
                gram.at[pl.ds(pl.multiple_of(q * strip, strip), strip)],
                pieces.at[it, e], red_sems.at[it, 0, e], red_sems.at[it, 1, e], peer_col(e),
            )

        def row_copy(d):
            place = strips.at[it, low_row]
            device = (group, base_row + lax.rem(low_row + d, low_rows), col)
            return remote(place, place, row_sems.at[it, 0, d], row_sems.at[it, 1, d], device)

        mine = pl.ds(pl.multiple_of(col * strip, strip), strip)

        def all_copy(e):
            place = whole.at[it, mine]
            return remote(place, place, all_sems.at[it, 0, e], all_sems.at[it, 1, e], peer_col(e))

        every(1, col_count, lambda e: red_copy(e).start())
        if last:
            for k in range(per):
                out_ref[k * block : (k + 1) * block, :] = app[it, col, k].T
        every(1, col_count, lambda e: red_copy(e).wait_recv())
        if not last:
            to_far[0].start()
            for k in range(per):
                to_near[k].start()
        summed = gram[mine, :]
        for e in range(1, col_count):
            summed = summed + pieces[it, e]
        strips[it, low_row] = summed
        every(1, low_rows, lambda d: row_copy(d).start())
        every(1, low_rows, lambda d: row_copy(d).wait_recv())
        summed = strips[it, 0]
        for d in range(1, low_rows):
            summed = summed + strips[it, d]
        step = 0
        while (1 << step) < high_rows:
            span = low_rows << step
            peer = row + span - 2 * span * lax.rem(row // span, 2)
            other[it, step, 0] = summed
            swap = remote(
                other.at[it, step, 0], other.at[it, step, 1],
                fly_sems.at[it, 0, step], fly_sems.at[it, 1, step], (group, peer, col),
            )
            swap.start()
            swap.wait()
            summed = summed + other[it, step, 1]
            step += 1
        whole[it, mine] = summed
        every(1, col_count, lambda e: all_copy(e).start())
        every(1, col_count, lambda e: all_copy(e).wait_recv())
        if not last:
            to_far[0].wait_recv()
            onward[0].start()
            for k in range(1, per):
                to_far[k].start()

        def pass_on():
            if not last:
                for k in range(1, per):
                    to_far[k].wait_recv()
                    onward[k].start()

        inverse = inverse_factor(whole[it] * (1.0 / total_cells), pass_on)
        every(1, col_count, lambda e: red_copy(e).wait_send())
        every(1, low_rows, lambda d: row_copy(d).wait_send())
        every(1, col_count, lambda e: all_copy(e).wait_send())
        first_half.wait_send()
        second_half.wait_send()
        over.wait_send()
        if not last:
            shares.wait_send()
        if last:
            inverse_ref[...] = inverse
        else:
            for k in range(per):
                to_near[k].wait_recv()
                onward[k].wait_recv()
                to_far[k].wait_send()
                to_near[k].wait_send()
                onward[k].wait_send()
            for b in range(blocks):
                vec[b] = jnp.dot(
                    inverse, app[it, b // per, b % per], precision=highest, preferred_element_type=f32
                ).astype(bf16)


def shards(block_tiles, block_rows, block_cols, counts, cell_order, start_vectors):
    row_count = lax.axis_size("rows")
    col_count = lax.axis_size("cols")
    stored = block_tiles.reshape(block_tiles.shape[1:])
    tile_count, block = stored.shape[0], stored.shape[1]
    cells = cell_order.shape[1]
    blocks = cells // block
    width = start_vectors.shape[1]
    per = blocks // col_count
    smem = pl.BlockSpec(memory_space=pltpu.SMEM)
    vmem = pl.BlockSpec(memory_space=pltpu.VMEM)
    low_rows = min(row_count, DIRECT)
    strip = width // col_count
    fly = max(1, (row_count // low_rows).bit_length() - 1)
    dma = pltpu.SemaphoreType.DMA
    applied, inverse = pl.pallas_call(
        functools.partial(sweep_kernel, row_count, col_count, cells * row_count),
        out_shape=(jax.ShapeDtypeStruct((per * block, width), f32), jax.ShapeDtypeStruct((width, width), f32)),
        in_specs=[vmem, vmem, smem, vmem, vmem, pl.BlockSpec(memory_space=pl.ANY)],
        out_specs=(vmem, vmem),
        scratch_shapes=[
            pltpu.VMEM((LINES, LANES), jnp.int32),
            pltpu.SMEM((LINES, LANES), jnp.int32),
            pltpu.VMEM((row_count, 8, block), jnp.int32),
            pltpu.VMEM((tile_count, block, block), bf16),
            pltpu.VMEM((tile_count + 1, width, block), f32),
            pltpu.VMEM((tile_count + 1, width, block), f32),
            pltpu.VMEM((blocks, width, block), bf16),
            pltpu.VMEM((col_count, per, width, block), f32),
            pltpu.VMEM((ITERS, col_count, per, width, block), f32),
            pltpu.VMEM((ITERS, row_count, width, block), bf16),
            pltpu.VMEM((ITERS, row_count, width, block), bf16),
            pltpu.VMEM((ITERS, row_count, width, block), bf16),
            pltpu.VMEM((ITERS, row_count, width, block), bf16),
            pltpu.VMEM((row_count, 8, block), jnp.int32),
            pltpu.VMEM((2, per, width, block), f32),
            pltpu.VMEM((col_count, per, width, block), bf16),
            pltpu.VMEM((ITERS, per, width, block), bf16),
            pltpu.VMEM((2, per, width, block), bf16),
            pltpu.VMEM((ITERS, per, width, block), bf16),
            pltpu.VMEM((width, width), f32),
            pltpu.VMEM((ITERS, col_count, strip, width), f32),
            pltpu.VMEM((ITERS, low_rows, strip, width), f32),
            pltpu.VMEM((ITERS, width, width), f32),
            pltpu.VMEM((ITERS, fly, 2, strip, width), f32),
            pltpu.VMEM((width, block), f32),
            pltpu.VMEM((per, 8, block), f32),
            pltpu.VMEM((per, 8, block), f32),
            dma,
            dma,
            dma((2,)),
            dma((2, row_count)),
            dma((ITERS, 2, row_count)),
            dma((ITERS, 2, row_count)),
            dma((ITERS, 2, 2)),
            dma((ITERS, 2)),
            dma((2, 3, per)),
            dma((ITERS, 2, col_count)),
            dma((ITERS, 2, low_rows)),
            dma((ITERS, 2, col_count)),
            dma((ITERS, 2, fly)),
        ],
        compiler_params=pltpu.CompilerParams(
            collective_id=0, has_side_effects=True, vmem_limit_bytes=56 * 1024 * 1024
        ),
    )(block_rows, block_cols, counts, cell_order.reshape(blocks, 1, block), start_vectors, stored)
    return lax.dot_general(
        applied, inverse, (((1,), (1,)), ((), ())), precision=highest, preferred_element_type=f32
    )


def solution(mesh):
    in_specs = (
        P(("groups", "rows"), "cols", None, None),
        P(("groups", "rows"), "cols"),
        P(("groups", "rows"), "cols"),
        P(("groups", "rows"), "cols"),
        P(("groups", "rows"), None),
        P(("groups", "rows"), None),
    )
    out_specs = P(("groups", "rows", "cols"), None)
    return jax.shard_map(shards, mesh=mesh, in_specs=in_specs, out_specs=out_specs, check_vma=False)
```

```python
import functools

import jax
import jax.numpy as jnp
from jax import lax
from jax.experimental import pallas as pl
from jax.experimental.pallas import tpu as pltpu
from jax.sharding import PartitionSpec as P

ITERS = 2
MESH = pl.DeviceIdType.MESH
DIRECT = 4
diag_shift = 3.0
highest = lax.Precision.HIGHEST
f32 = jnp.float32
bf16 = jnp.bfloat16

F_TILE, F_IN, F_KEEP, G_TILE, G_IN, G_KEEP, F_LAST, G_LAST, R_TILE, R_ROW = range(10)


LINES = 16
LANES = 128


def route(row_count, blocks, own_row, rows_ref, cols_ref, counts_ref, lines_ref, want_ref):
    tiles = rows_ref.shape[1]
    i32 = jnp.int32
    square = (tiles, tiles)
    this = lax.broadcasted_iota(i32, square, 0)
    that = lax.broadcasted_iota(i32, square, 1)
    tile = lax.broadcasted_iota(i32, (tiles, LANES), 0)
    lane = lax.broadcasted_iota(i32, (tiles, LANES), 1)

    def count(flags, axis):
        return jnp.sum(jnp.where(flags, 1, 0), axis=axis, keepdims=True)

    def upright(line):
        return jnp.sum(jnp.where(this == that, jnp.broadcast_to(line, square), 0), axis=1, keepdims=True)

    def pick(flags, value):
        return jnp.sum(jnp.where(flags, value, 0), axis=0, keepdims=True)

    cols = cols_ref[...]
    owner = jnp.zeros(cols.shape, i32)
    for o in range(1, row_count):
        owner = owner + jnp.where(cols >= o * blocks, 1, 0)
    a = rows_ref[...] - own_row * blocks
    b = cols - owner * blocks
    live = jnp.where(lax.broadcasted_iota(i32, cols.shape, 1) < counts_ref[0, 0], 1, 0)
    local = jnp.where(owner == own_row, 1, 0)
    near = live * local
    for key, source, lines in ((a, b, (F_TILE, F_IN, F_KEEP, F_LAST)), (b, a, (G_TILE, G_IN, G_KEEP, G_LAST))):
        key = jnp.where(near > 0, key, blocks)
        own_key = upright(key)
        other = jnp.broadcast_to(key, square)
        equal = jnp.logical_and(other == own_key, that < this)
        seen = count(equal, 1)
        rank = count(other < own_key, 1) + seen
        here = rank == lane
        lines_ref[lines[0] : lines[0] + 1, :] = pick(here, tile)
        lines_ref[lines[1] : lines[1] + 1, :] = pick(here, upright(source * near))
        lines_ref[lines[2] : lines[2] + 1, :] = pick(here, jnp.minimum(seen, 1))
        lines_ref[lines[3] : lines[3] + 1, :] = jnp.where(count(own_key == lane, 0) > 0, count(own_key <= lane, 0), 0)
    far = jnp.logical_and(upright(owner) == lane, upright(live * (1 - local)) > 0)
    lines_ref[R_TILE : R_TILE + 1, :] = pick(far, tile)
    lines_ref[R_ROW : R_ROW + 1, :] = pick(far, upright(a) + 1) - 1
    want = pick(far, upright(b) + 1) - 1
    for o in range(row_count):
        want_ref[o] = jnp.broadcast_to(want[:, o : o + 1], want_ref.shape[1:])


def inverse_factor(gram, aside):
    size = gram.shape[0]
    panels = size // 8
    lanes = lax.broadcasted_iota(jnp.int32, (8, size), 1)
    subs = lax.broadcasted_iota(jnp.int32, (8, size), 0)
    g = [gram[8 * r : 8 * r + 8, :] for r in range(panels)]
    w = [(lanes == subs + 8 * r).astype(f32) for r in range(panels)]
    done = []
    phase = 4

    def spread(x, j):
        return jnp.broadcast_to(x[j : j + 1, :], (8, size))

    def panel(i, carry):
        g, w = list(carry[0]), list(carry[1])
        n = len(g)
        p, q = jnp.where(lanes < size - 8 * i, g[0], 0.0), w[0]
        col = [jnp.broadcast_to(p[:, m : m + 1], (8, size)) for m in range(8)]
        pivots = jnp.ones((8, size), f32)
        for j in range(0, 8, 2):
            k = j + 1
            one, low, up, two = spread(col[j], j), spread(col[j], k), spread(col[k], j), spread(col[k], k)
            det = one * two - low * up
            inv = 1.0 / one
            inv_det = 1.0 / det
            step = low * inv
            pivots = jnp.where(subs == j, one, jnp.where(subs == k, det * inv, pivots))
            first = jnp.where(subs > j, col[j] * inv, 0.0)
            second = jnp.where(subs > k, (col[k] - first * up) * (one * inv_det), 0.0)

            def clear(x):
                top = spread(x, j)
                return x - first * top - second * (spread(x, k) - step * top)

            for m in range(j + 2, 8):
                col[m] = clear(col[m])
            p, q = clear(p), clear(q)
        factors = jnp.transpose(p / pivots)
        p_rows = [spread(p, j) for j in range(8)]
        q_rows = [spread(q, j) for j in range(8)]
        for r in range(1, n):
            for j in range(8):
                mult = jnp.broadcast_to(factors[8 * r : 8 * r + 8, j : j + 1], (8, size))
                g[r] = g[r] - mult * p_rows[j]
                w[r] = w[r] - mult * q_rows[j]
        g = [pltpu.roll(g[r], size - 8, 1) for r in range(1, n)] + [jnp.zeros((8, size), f32)]
        w = w[1:] + [q * lax.rsqrt(pivots)]
        return tuple(g), tuple(w)

    at = 0
    while g:
        steps = min(phase, len(g))
        g, w = lax.fori_loop(at, at + steps, panel, (tuple(g), tuple(w)))
        g, w = list(g), list(w)
        at += steps
        if len(g) == 2 * phase:
            aside()
        keep = len(g) - steps
        done += w[keep:]
        g, w = g[:keep], w[:keep]
    return jnp.concatenate(done, axis=0)


def sweep_kernel(
    row_count, col_count, total_cells,
    rows_ref, cols_ref, counts_ref, order_ref, start_ref, tiles_hbm, out_ref, inverse_ref,
    lines_ref, tab_ref, want_ref,
    tiles, near_f, near_g, vec, part, app, answer, outgoing, fetched, returned, asked,
    half, part16, mid16, half16, cross16, gram, pieces, strips, whole, other, common, share, shared,
    tile_sem, tab_sem, share_sems, id_sems, ans_sems, ret_sems, half_sems, cross_sems, gat_sems, red_sems, row_sems, all_sems, fly_sems,
):
    group = lax.axis_index("groups")
    row = lax.axis_index("rows")
    col = lax.axis_index("cols")
    blocks, width, block = vec.shape
    per = blocks // col_count
    tile_count = tiles.shape[0]
    low_rows = min(row_count, DIRECT)
    high_rows = row_count // low_rows
    strip = width // col_count
    near_col = col + 1 - 2 * lax.rem(col, 2)
    far_col = lax.rem(col + 2, 4)
    base_row = (row // low_rows) * low_rows
    low_row = row - base_row

    def every(first, last, body):
        if last - first <= 16:
            for d in reversed(range(first, last)):
                body(d)
        else:
            lax.fori_loop(first, last, lambda d, c: (body(d), c)[1], 0)

    def remote(src, dst, send, recv, device):
        return pltpu.make_async_remote_copy(
            src_ref=src, dst_ref=dst, send_sem=send, recv_sem=recv, device_id=device, device_id_type=MESH
        )

    load = pltpu.make_async_copy(tiles_hbm, tiles, tile_sem)
    load.start()

    barrier = pltpu.get_barrier_semaphore()

    def greet_row(d):
        pl.semaphore_signal(
            barrier, inc=1, device_id=(group, lax.rem(row + d, row_count), col), device_id_type=MESH
        )

    def greet_col(e):
        pl.semaphore_signal(
            barrier, inc=1, device_id=(group, row, lax.rem(col + e, col_count)), device_id_type=MESH
        )

    every(1, row_count, greet_row)
    every(1, col_count, greet_col)
    route(row_count, blocks, row, rows_ref, cols_ref, counts_ref, lines_ref, want_ref)
    table = pltpu.make_async_copy(lines_ref, tab_ref, tab_sem)
    table.start()
    first = start_ref[...].astype(f32).T.astype(bf16)
    cells = first.shape[1]

    def permute(b, _):
        hit = lax.broadcasted_iota(jnp.int32, (cells, block), 0) == order_ref[b]
        vec[b] = jnp.dot(first, hit.astype(f32).astype(bf16), preferred_element_type=f32).astype(bf16)
        return 0

    lax.fori_loop(0, blocks, permute, 0)
    mean = vec[0].astype(f32)
    for b in range(1, blocks):
        mean = mean + vec[b].astype(f32)
    mean = jnp.sum(mean, axis=1, keepdims=True) * (1.0 / cells)
    scale = lax.rsqrt(jnp.maximum(jnp.sum(mean * mean, axis=0, keepdims=True), 1e-30))
    common[...] = jnp.broadcast_to(mean * scale, common.shape)

    pl.semaphore_wait(barrier, (row_count - 1) + (col_count - 1))

    def up(d):
        return (group, row + d, col)

    def down(d):
        return (group, row - d, col)

    def id_copy(d, device):
        return remote(want_ref.at[lax.rem(row + d, row_count)], asked.at[d], id_sems.at[0, d], id_sems.at[1, d], device)

    def send_ids(d):
        @pl.when(row + d < row_count)
        def _():
            id_copy(d, up(d)).start()

    every(1, row_count, send_ids)

    near_f[0] = jnp.zeros((width, block), f32)
    near_g[0] = jnp.zeros((width, block), f32)

    def finish_ids(d):
        @pl.when(row + d < row_count)
        def _():
            id_copy(d, up(d)).wait_send()

        @pl.when(row - d >= 0)
        def _():
            id_copy(d, up(d)).wait_recv()

    table.wait()
    load.wait()

    for it in range(ITERS):

        def ans_copy(d):
            return remote(answer.at[it, d], fetched.at[it, d], ans_sems.at[it, 0, d], ans_sems.at[it, 1, d], down(d))

        def ret_copy(d):
            return remote(outgoing.at[it, d], returned.at[it, d], ret_sems.at[it, 0, d], ret_sems.at[it, 1, d], up(d))

        def send_down(d):
            @pl.when(row - d >= 0)
            def _():
                ids = asked[d][0:1, :]
                found = jnp.zeros((width, block), f32)
                for b in range(blocks):
                    found = jnp.where(ids == b, vec[b].astype(f32), found)
                answer[it, d] = found.astype(bf16)
                ans_copy(d).start()

        def send_up(d):
            @pl.when(row + d < row_count)
            def _():
                peer = row + d
                a = jnp.maximum(tab_ref[R_ROW, peer], 0)
                outgoing[it, d] = jnp.dot(vec[a], tiles[tab_ref[R_TILE, peer]], preferred_element_type=f32).astype(bf16)
                ret_copy(d).start()

        every(1, row_count, send_up)
        if it > 0:
            every(1, row_count, send_down)

        def near(i, _):
            ahead = lax.dot_general(
                vec[tab_ref[F_IN, i]], tiles[tab_ref[F_TILE, i]], (((1,), (1,)), ((), ())), preferred_element_type=f32
            )
            near_f[i + 1] = near_f[i] * tab_ref[F_KEEP, i].astype(f32) + ahead
            back = jnp.dot(vec[tab_ref[G_IN, i]], tiles[tab_ref[G_TILE, i]], preferred_element_type=f32)
            near_g[i + 1] = near_g[i] * tab_ref[G_KEEP, i].astype(f32) + back.astype(bf16).astype(f32)
            return 0

        early = tile_count // 4 if it == 0 else 0
        if it == 0:
            lax.fori_loop(0, early, near, 0, unroll=2)
            every(1, row_count, finish_ids)
            every(1, row_count, send_down)
        lax.fori_loop(early, tile_count, near, 0, unroll=2)
        for b in range(blocks):
            part[b // per, b % per] = near_f[tab_ref[F_LAST, b]] + near_g[tab_ref[G_LAST, b]]

        def take_far(d):
            @pl.when(row + d < row_count)
            def _():
                peer = row + d
                ret_copy(d).wait_send()
                ans_copy(d).wait_recv()
                ahead = lax.dot_general(
                    fetched[it, d], tiles[tab_ref[R_TILE, peer]], (((1,), (1,)), ((), ())), preferred_element_type=f32
                )
                a = tab_ref[R_ROW, peer]
                for b in range(blocks):
                    part[b // per, b % per] += ahead * (a == b).astype(f32)

            @pl.when(row - d >= 0)
            def _():
                ans_copy(d).wait_send()
                ret_copy(d).wait_recv()
                ids = asked[d][0:1, :]
                back = returned[it, d].astype(f32)
                for b in range(blocks):
                    part[b // per, b % per] += jnp.where(ids == b, back, 0.0)

        every(1, row_count, take_far)

        last = it == ITERS - 1
        near_dev = (group, row, near_col)
        far_dev = (group, row, far_col)
        near_far = lax.rem(near_col + 2, 4)
        if last:
            part16[near_far] = part[near_far].astype(bf16)
            part16[near_col] = part[near_col].astype(bf16)
        out, arrived = (part16, half16) if last else (part, half)
        sent, crossed = mid16.at[it], cross16.at[it]
        shares = remote(share, shared, share_sems.at[0], share_sems.at[1], far_dev)
        first_half = [
            remote(out.at[near_far, k], arrived.at[0, k], half_sems.at[it, 0, k], half_sems.at[it, 1, k], near_dev)
            for k in range(per)
        ]
        second_half = remote(
            out.at[near_col], arrived.at[1], half_sems.at[it, 0, per], half_sems.at[it, 1, per], near_dev
        )
        over = [
            remote(sent.at[k], crossed.at[k], cross_sems.at[it, 0, k], cross_sems.at[it, 1, k], far_dev)
            for k in range(per)
        ]
        for k in range(per):
            first_half[k].start()
        second_half.start()
        for k in range(per):
            first_half[k].wait_recv()
            value = part[far_col, k] + arrived[0, k].astype(f32)
            if not last:
                along = jnp.sum(common[...] * value, axis=0, keepdims=True)
                share[k] = jnp.broadcast_to(along, share.shape[1:])
                value = value - common[...] * along
            sent[k] = value.astype(bf16)
            over[k].start()
        if not last:
            shares.start()
        second_half.wait_recv()
        own = part[col] + arrived[1].astype(f32)
        for k in range(per):
            part[col, k] = own[k] + diag_shift * vec[col * per + k].astype(f32)
        if not last:
            shares.wait_recv()
        for k in range(per):
            over[k].wait_recv()
            piece = part[col, k] + crossed[k].astype(f32)
            if not last:
                piece = piece + common[...] * shared[k, 0:1, :]
            app[it, col, k] = piece

        def gat_copy(kind, k, quarter, device):
            place = app.at[it, quarter, k]
            return remote(place, place, gat_sems.at[0, kind, k], gat_sems.at[1, kind, k], device)

        to_far = [gat_copy(0, k, col, far_dev) for k in range(per)]
        to_near = [gat_copy(1, k, col, near_dev) for k in range(per)]
        onward = [gat_copy(2, k, far_col, near_dev) for k in range(per)]
        total = jnp.zeros((width, width), f32)
        for k in range(per):
            piece = app[it, col, k]
            total = total + lax.dot_general(
                piece, piece, (((1,), (1,)), ((), ())), precision=highest, preferred_element_type=f32
            )
        gram[...] = total

        def peer_col(e):
            return (group, row, lax.rem(col + e, col_count))

        def red_copy(e):
            q = lax.rem(col + e, col_count)
            return remote(
                gram.at[pl.ds(pl.multiple_of(q * strip, strip), strip)],
                pieces.at[it, e], red_sems.at[it, 0, e], red_sems.at[it, 1, e], peer_col(e),
            )

        def row_copy(d):
            place = strips.at[it, low_row]
            device = (group, base_row + lax.rem(low_row + d, low_rows), col)
            return remote(place, place, row_sems.at[it, 0, d], row_sems.at[it, 1, d], device)

        mine = pl.ds(pl.multiple_of(col * strip, strip), strip)

        def all_copy(e):
            place = whole.at[it, mine]
            return remote(place, place, all_sems.at[it, 0, e], all_sems.at[it, 1, e], peer_col(e))

        every(1, col_count, lambda e: red_copy(e).start())
        if last:
            for k in range(per):
                out_ref[k * block : (k + 1) * block, :] = app[it, col, k].T
        every(1, col_count, lambda e: red_copy(e).wait_recv())
        if not last:
            to_far[0].start()
            for k in range(per):
                to_near[k].start()
        summed = gram[mine, :]
        for e in range(1, col_count):
            summed = summed + pieces[it, e]
        strips[it, low_row] = summed
        every(1, low_rows, lambda d: row_copy(d).start())
        every(1, low_rows, lambda d: row_copy(d).wait_recv())
        summed = strips[it, 0]
        for d in range(1, low_rows):
            summed = summed + strips[it, d]
        step = 0
        while (1 << step) < high_rows:
            span = low_rows << step
            peer = row + span - 2 * span * lax.rem(row // span, 2)
            other[it, step, 0] = summed
            swap = remote(
                other.at[it, step, 0], other.at[it, step, 1],
                fly_sems.at[it, 0, step], fly_sems.at[it, 1, step], (group, peer, col),
            )
            swap.start()
            swap.wait()
            summed = summed + other[it, step, 1]
            step += 1
        whole[it, mine] = summed
        every(1, col_count, lambda e: all_copy(e).start())
        every(1, col_count, lambda e: all_copy(e).wait_recv())
        if not last:
            to_far[0].wait_recv()
            onward[0].start()
            for k in range(1, per):
                to_far[k].start()

        def pass_on():
            if not last:
                for k in range(1, per):
                    to_far[k].wait_recv()
                    onward[k].start()

        inverse = inverse_factor(whole[it] * (1.0 / total_cells), pass_on)
        every(1, col_count, lambda e: red_copy(e).wait_send())
        every(1, low_rows, lambda d: row_copy(d).wait_send())
        every(1, col_count, lambda e: all_copy(e).wait_send())
        second_half.wait_send()
        for k in range(per):
            first_half[k].wait_send()
            over[k].wait_send()
        if not last:
            shares.wait_send()
        if last:
            inverse_ref[...] = inverse
        else:
            for k in range(per):
                to_near[k].wait_recv()
                onward[k].wait_recv()
                to_far[k].wait_send()
                to_near[k].wait_send()
                onward[k].wait_send()
            for b in range(blocks):
                vec[b] = jnp.dot(
                    inverse, app[it, b // per, b % per], precision=highest, preferred_element_type=f32
                ).astype(bf16)


def shards(block_tiles, block_rows, block_cols, counts, cell_order, start_vectors):
    row_count = lax.axis_size("rows")
    col_count = lax.axis_size("cols")
    stored = block_tiles.reshape(block_tiles.shape[1:])
    tile_count, block = stored.shape[0], stored.shape[1]
    cells = cell_order.shape[1]
    blocks = cells // block
    width = start_vectors.shape[1]
    per = blocks // col_count
    smem = pl.BlockSpec(memory_space=pltpu.SMEM)
    vmem = pl.BlockSpec(memory_space=pltpu.VMEM)
    low_rows = min(row_count, DIRECT)
    strip = width // col_count
    fly = max(1, (row_count // low_rows).bit_length() - 1)
    dma = pltpu.SemaphoreType.DMA
    applied, inverse = pl.pallas_call(
        functools.partial(sweep_kernel, row_count, col_count, cells * row_count),
        out_shape=(jax.ShapeDtypeStruct((per * block, width), f32), jax.ShapeDtypeStruct((width, width), f32)),
        in_specs=[vmem, vmem, smem, vmem, vmem, pl.BlockSpec(memory_space=pl.ANY)],
        out_specs=(vmem, vmem),
        scratch_shapes=[
            pltpu.VMEM((LINES, LANES), jnp.int32),
            pltpu.SMEM((LINES, LANES), jnp.int32),
            pltpu.VMEM((row_count, 8, block), jnp.int32),
            pltpu.VMEM((tile_count, block, block), bf16),
            pltpu.VMEM((tile_count + 1, width, block), f32),
            pltpu.VMEM((tile_count + 1, width, block), f32),
            pltpu.VMEM((blocks, width, block), bf16),
            pltpu.VMEM((col_count, per, width, block), f32),
            pltpu.VMEM((ITERS, col_count, per, width, block), f32),
            pltpu.VMEM((ITERS, row_count, width, block), bf16),
            pltpu.VMEM((ITERS, row_count, width, block), bf16),
            pltpu.VMEM((ITERS, row_count, width, block), bf16),
            pltpu.VMEM((ITERS, row_count, width, block), bf16),
            pltpu.VMEM((row_count, 8, block), jnp.int32),
            pltpu.VMEM((2, per, width, block), f32),
            pltpu.VMEM((col_count, per, width, block), bf16),
            pltpu.VMEM((ITERS, per, width, block), bf16),
            pltpu.VMEM((2, per, width, block), bf16),
            pltpu.VMEM((ITERS, per, width, block), bf16),
            pltpu.VMEM((width, width), f32),
            pltpu.VMEM((ITERS, col_count, strip, width), f32),
            pltpu.VMEM((ITERS, low_rows, strip, width), f32),
            pltpu.VMEM((ITERS, width, width), f32),
            pltpu.VMEM((ITERS, fly, 2, strip, width), f32),
            pltpu.VMEM((width, block), f32),
            pltpu.VMEM((per, 8, block), f32),
            pltpu.VMEM((per, 8, block), f32),
            dma,
            dma,
            dma((2,)),
            dma((2, row_count)),
            dma((ITERS, 2, row_count)),
            dma((ITERS, 2, row_count)),
            dma((ITERS, 2, per + 1)),
            dma((ITERS, 2, per)),
            dma((2, 3, per)),
            dma((ITERS, 2, col_count)),
            dma((ITERS, 2, low_rows)),
            dma((ITERS, 2, col_count)),
            dma((ITERS, 2, fly)),
        ],
        compiler_params=pltpu.CompilerParams(
            collective_id=0, has_side_effects=True, vmem_limit_bytes=56 * 1024 * 1024
        ),
    )(block_rows, block_cols, counts, cell_order.reshape(blocks, 1, block), start_vectors, stored)
    return lax.dot_general(
        applied, inverse, (((1,), (1,)), ((), ())), precision=highest, preferred_element_type=f32
    )


def solution(mesh):
    in_specs = (
        P(("groups", "rows"), "cols", None, None),
        P(("groups", "rows"), "cols"),
        P(("groups", "rows"), "cols"),
        P(("groups", "rows"), "cols"),
        P(("groups", "rows"), None),
        P(("groups", "rows"), None),
    )
    out_specs = P(("groups", "rows", "cols"), None)
    return jax.shard_map(shards, mesh=mesh, in_specs=in_specs, out_specs=out_specs, check_vma=False)
```
